128 devices in a mesh: section: 16 (over y, x_lo, core), narrow: 8 (over z, x_hi).
Axes of the slice: x: 4 (x_hi: 2, x_lo: 2; x = x_hi * 2 + x_lo), y: 4, z: 4, core: 2. Of those that a mesh axis runs over, the one named last changes fastest.
Arguments:
- tokens: bfloat16 [16384, 4096], P(('section', 'narrow')), may hold values from -6 to 6
- upstream: bfloat16 [16384, 4096], P(('section', 'narrow')), may hold values from -6 to 6
- up_weight: bfloat16 [8, 4096, 8192], P('narrow', None, 'section'), may hold values from -0.09375 to 0.09375
- down_weight: bfloat16 [8, 8192, 4096], P('narrow', 'section'), may hold values from -0.0625 to 0.0625
- gate_values: float32 [8, 512], P('narrow', 'section'), may hold values from 0.2 to 1
- chosen: int32 [8, 512], P(None, 'section'), may hold values from 0 to 16383, as said below
- counts: int32 [8, 16], P(None, 'section'), may hold values from 0 to 32, as said below
Outputs:
- layer_out: bfloat16 [16384, 4096], P(('section', 'narrow'))
- token_grad: bfloat16 [16384, 4096], P(('section', 'narrow'))
- up_grad: bfloat16 [8, 4096, 8192], P('narrow', None, 'section')
- down_grad: bfloat16 [8, 8192, 4096], P('narrow', 'section')
- gate_grad: float32 [8, 512], P('narrow', 'section')
The draws below stay inside these ranges and needn't reach their ends.
Inputs may be any that keep to these rules, and one draw needn't show every extreme that they name: `chosen`: block g of each expert's list (slots g * 32 to (g + 1) * 32 - 1) names 32 different tokens of routing group g, the tokens g * 1024 to (g + 1) * 1024 - 1. counts[e, g] live slots lead block g of expert e's list; the others are ignored. Every expert has one full block.
All inputs are finite; a program needn't handle non-finite values.
Results may differ from the reference program's by a relative error of at most 0.025.
Values may be sent and summed in bfloat16 or wider, within the bound.
No kernel may reach another device: no remote copies, remote signals or barrier semaphores. Data moves between devices by JAX's collectives and lax.ppermute only.
A program may use at most 128 MiB of HBM per device.

```python
import jax
import jax.numpy as jnp
from jax import lax

D = 4096
H = 8192
E = 8
GROUP = 1024
CB = 32
C = 512
TOKENS = 16384
N_SECTION = 16


def draw_chosen(key, part):
    key = jax.random.fold_in(key, 11)
    keys = jax.random.split(key, E * N_SECTION)
    picks = jax.vmap(lambda sub_key: jax.random.permutation(sub_key, GROUP)[:CB])(keys)
    offsets = jnp.arange(E * N_SECTION, dtype=jnp.int32) % N_SECTION * GROUP
    return (picks.astype(jnp.int32) + offsets[:, None]).reshape(E, C)


def draw_counts(key, part):
    key = jax.random.fold_in(key, 23)
    first_key, second_key, third_key = jax.random.split(key, 3)
    uniform_draw = jax.random.randint(first_key, (E, N_SECTION), 0, CB + 1)
    levels = jax.random.randint(second_key, (E, 1), 1, 5)
    scaled = jnp.minimum(CB, uniform_draw * levels // 2)
    full_at = jax.random.randint(third_key, (E, 1), 0, N_SECTION)
    column = jnp.arange(N_SECTION, dtype=jnp.int32)[None, :]
    return jnp.where(column == full_at, CB, scaled).astype(jnp.int32)


def level_of(key, dims, pieces, smallest, high):
    level = 1.0
    for axis_at, blocks in pieces:
        steps = jax.random.uniform(jax.random.fold_in(jax.random.fold_in(key, 6), axis_at), (blocks,), jnp.float32, smallest / len(pieces), high / len(pieces))
        level = level * jnp.repeat(jnp.exp(steps), dims[axis_at] // blocks).reshape((-1,) + (1,) * (len(dims) - 1 - axis_at))
    return level


def gaussian(stream_key, extent, scale, limit, shards=(), kind=jnp.bfloat16):
    values = scale * jax.random.normal(stream_key, extent, jnp.float32)
    if shards:
        values = values * level_of(stream_key, extent, shards, -0.22, 0.18)
    return jnp.clip(values, -limit, limit).astype(kind)


def setup_inputs(seed: int = 0) -> dict:
    seeds = jax.random.split(jax.random.key(seed), 8)
    tokens = gaussian(seeds[0], (TOKENS, D), 1.0, 6.0, ((0, 128),))
    upstream = gaussian(seeds[1], (TOKENS, D), 1.0, 6.0, ((0, 128),))
    up_weight = gaussian(seeds[2], (E, D, H), D ** -0.5, 0.09375, ((0, 8), (2, 16)))
    down_weight = gaussian(seeds[3], (E, H, D), H ** -0.5, 0.0625, ((0, 8), (1, 16)))
    gate_values = jnp.clip(0.2 + 0.8 * jax.random.uniform(seeds[4], (E, C), jnp.float32) ** level_of(seeds[4], (E, C), ((0, 8), (1, 16)), -0.2, 0.2), 0.2, 1.0)
    chosen = draw_chosen(jax.random.fold_in(seeds[7], 71), 0)
    counts = draw_counts(jax.random.fold_in(seeds[7], 71), 0)
    return {"tokens": tokens, "upstream": upstream, "up_weight": up_weight, "down_weight": down_weight, "gate_values": gate_values, "chosen": chosen, "counts": counts}


def gelu_tanh(values):
    return jax.nn.gelu(values, approximate=True)

def round_partial(values):
    narrowed = lax.optimization_barrier(values.astype(jnp.bfloat16))
    return narrowed.astype(jnp.float32)

def block_sum(left, right):
    block_width = H // N_SECTION
    total = jnp.zeros((left.shape[0], right.shape[1]), jnp.float32)
    for block_index in range(N_SECTION):
        offset = block_index * block_width
        partial_sum = jnp.dot(left[:, offset:offset + block_width], right[offset:offset + block_width], preferred_element_type=jnp.float32)
        total = total + round_partial(partial_sum)
    return total

def one_expert(operands, tokens, upstream):
    up_matrix, down_matrix, gate_row, chosen_row, count_row = operands
    slot_index = jnp.arange(C, dtype=jnp.int32)
    alive_mask = slot_index % CB < count_row[slot_index // CB]
    picked = jnp.where(alive_mask[:, None], tokens[chosen_row], 0).astype(jnp.bfloat16)
    pre_act = jnp.dot(picked, up_matrix, preferred_element_type=jnp.float32)
    hidden = gelu_tanh(pre_act).astype(jnp.bfloat16)
    out_sum = block_sum(hidden, down_matrix)
    contrib = jnp.where(alive_mask[:, None], gate_row[:, None] * out_sum, 0.0).astype(jnp.bfloat16)
    back_rows = jnp.where(alive_mask[:, None], upstream[chosen_row], 0).astype(jnp.bfloat16)
    gate_grad = lax.optimization_barrier(jnp.sum(back_rows.astype(jnp.float32) * out_sum, axis=1))
    out_grad = (gate_row[:, None] * back_rows.astype(jnp.float32)).astype(jnp.bfloat16)
    down_grad = jnp.dot(hidden.T, out_grad, preferred_element_type=jnp.float32).astype(jnp.bfloat16)
    act_grad = jnp.dot(out_grad, down_matrix.T, preferred_element_type=jnp.float32)
    unused_value, pull_back = jax.vjp(gelu_tanh, pre_act)
    pre_grad = pull_back(act_grad)[0].astype(jnp.bfloat16)
    up_grad = jnp.dot(picked.T, pre_grad, preferred_element_type=jnp.float32).astype(jnp.bfloat16)
    picked_grad = block_sum(pre_grad, up_matrix.T).astype(jnp.bfloat16)
    return (contrib, picked_grad, up_grad, down_grad, gate_grad)

def reference(tokens, upstream, up_weight, down_weight, gate_values, chosen, counts):

    def expert_step(operands):
        return one_expert(operands, tokens, upstream)
    contrib, picked_grad, up_grad, down_grad, gate_grad = lax.map(expert_step, (up_weight, down_weight, gate_values, chosen, counts))
    flat_ids = chosen.reshape(-1)
    layer_out = jnp.zeros((TOKENS, D), jnp.float32).at[flat_ids].add(contrib.reshape(-1, D).astype(jnp.float32))
    token_grad = jnp.zeros((TOKENS, D), jnp.float32).at[flat_ids].add(picked_grad.reshape(-1, D).astype(jnp.float32))
    return (layer_out.astype(jnp.bfloat16), token_grad.astype(jnp.bfloat16), up_grad, down_grad, gate_grad)
```

```python
import jax
import jax.numpy as jnp
from jax import lax
from jax.sharding import Mesh, PartitionSpec as P

Y, XL, CORE, Z, XH = "y", "xl", "c", "z", "xh"
BF16 = jnp.bfloat16
F32 = jnp.float32
SPREAD = "pp"


def shift(value, axis, by):
    n = lax.axis_size(axis)
    return lax.ppermute(value, axis, [(i, (i + by) % n) for i in range(n)])


def add(*terms):
    total = terms[0].astype(F32)
    for term in terms[1:]:
        total = total + term.astype(F32)
    return total


def scatter_sum(q, ring, pair):
    from_pair = shift(q[2][1], pair, 1)
    two = add(q[2][0], from_pair).astype(BF16)
    got_two = shift(two, ring, -1)
    got_up = shift(q[1][1], ring, 1)
    got_pair = shift(q[3][1], pair, 1)
    near = add(q[0][1], got_up).astype(BF16)
    below = add(q[3][0], got_two, got_pair).astype(BF16)
    last_up = shift(q[1][0], ring, 1)
    last_pair = shift(near, pair, 1)
    last_down = shift(below, ring, -1)
    return add(q[0][0], last_up, last_pair, last_down)


def gather(own, ring, pair):
    r01 = shift(own, pair, 1)
    r10 = shift(own, ring, -1)
    r30 = shift(own, ring, 1)
    r20 = shift(r30, ring, 1)
    r11 = shift(r01, ring, -1)
    r31 = shift(r30, pair, 1)
    r21 = shift(r20, pair, 1)
    return [[own, r01], [r10, r11], [r20, r21], [r30, r31]]


def flat(rows):
    return [value for row in rows for value in row]


def relative(table, ring, pair):
    double = jnp.concatenate([table, table], axis=0)
    turned = lax.dynamic_slice_in_dim(double, lax.axis_index(ring), 4, axis=0)
    return jnp.where(lax.axis_index(pair) == 1, turned[:, ::-1], turned)


def gelu_tanh(values):
    return jax.nn.gelu(values, approximate=True)


def shards(tokens, upstream, up_weight, down_weight, gate_values, chosen, counts):
    section_id = lax.axis_index((Y, XL, CORE))
    narrow_id = lax.axis_index((Z, XH))
    tok_dev = tokens.shape[0]
    experts, slots = chosen.shape
    width = tokens.shape[1]
    up_local = up_weight[0]
    down_local = down_weight[0]
    gate_column = gate_values[0][:, None]
    alive = lax.broadcasted_iota(jnp.int32, (experts, slots), 1) < counts
    place = jnp.where(alive, chosen - section_id * (tok_dev * experts), -1)
    place = relative(place.reshape(4, 2, slots), Z, XH).reshape(experts * slots)
    mine_alive = place[:slots] >= 0
    own_select = (
        (place - narrow_id * tok_dev)[:, None] == lax.broadcasted_iota(jnp.int32, (1, tok_dev), 1)
    ) & (place >= 0)[:, None]
    own_select = own_select.astype(BF16)

    def blocks(array):
        return [[array[(2 * i + j) * slots:(2 * i + j + 1) * slots] for j in range(2)] for i in range(4)]

    def collect(source):
        picks = jnp.dot(own_select, source, preferred_element_type=F32).astype(BF16)
        return scatter_sum(blocks(picks), Z, XH).astype(BF16)

    def deliver(slot_values):
        every = jnp.concatenate(flat(gather(slot_values, Z, XH)), axis=0)
        return lax.dot_general(
            own_select, every, (((0,), (0,)), ((), ())), preferred_element_type=F32
        ).astype(BF16)

    def spread(slot_values):
        if SPREAD == "sc":
            return lax.all_gather(slot_values, (Y, XL, CORE), axis=0, tiled=True)
        half = jnp.concatenate(flat(gather(slot_values, Y, XL)), axis=0)
        return jnp.concatenate([half, shift(half, CORE, 1)], axis=0)

    def own_first(values):
        if SPREAD != "sc":
            return values
        table = values.reshape(4, 2, 2, slots * values.shape[1])
        table = jnp.where(lax.axis_index(CORE) == 1, table[:, :, ::-1], table)
        table = relative(table, Y, XL).transpose(2, 0, 1, 3)
        return table.reshape(values.shape)

    def hidden_sum(left, right, contract):
        left = own_first(left)
        half = left.shape[0] // 2
        dims = (((1,), (contract,)), ((), ()))
        other = lax.dot_general(left[half:], right, dims, preferred_element_type=F32).astype(BF16)
        here = lax.dot_general(left[:half], right, dims, preferred_element_type=F32)
        here = add(here, shift(other, CORE, 1)).astype(BF16)
        return scatter_sum(blocks(here), Y, XL)

    picked_all = spread(collect(tokens))
    back_mine = collect(upstream)
    back_wide = back_mine.astype(F32)
    out_grad_all = spread((gate_column * back_wide).astype(BF16))
    pre_act = jnp.dot(picked_all, up_local, preferred_element_type=F32)
    hidden = gelu_tanh(pre_act).astype(BF16)
    out_sum = hidden_sum(hidden, down_local, 0)
    contrib = jnp.where(mine_alive[:, None], gate_column * out_sum, 0.0).astype(BF16)
    gate_grad = jnp.sum(back_wide * out_sum, axis=1)[None, :]
    layer_out = deliver(contrib)
    act_grad = lax.dot_general(
        out_grad_all, down_local, (((1,), (1,)), ((), ())), preferred_element_type=F32
    )
    unused_value, pull_back = jax.vjp(gelu_tanh, pre_act)
    pre_grad = pull_back(act_grad)[0].astype(BF16)
    picked_grad = hidden_sum(pre_grad, up_local, 1).astype(BF16)
    token_grad = deliver(picked_grad)
    down_grad = lax.dot_general(
        hidden, out_grad_all, (((0,), (0,)), ((), ())), preferred_element_type=F32
    ).astype(BF16)
    up_grad = lax.dot_general(
        picked_all, pre_grad, (((0,), (0,)), ((), ())), preferred_element_type=F32
    ).astype(BF16)
    return (layer_out, token_grad, up_grad[None], down_grad[None], gate_grad)


def solution(mesh):
    fine = Mesh(mesh.devices.reshape(4, 2, 2, 4, 2), (Y, XL, CORE, Z, XH))
    section, narrow = (Y, XL, CORE), (Z, XH)
    return jax.shard_map(
        shards,
        mesh=fine,
        in_specs=(
            P(section + narrow, None),
            P(section + narrow, None),
            P(narrow, None, section),
            P(narrow, section, None),
            P(narrow, section),
            P(None, section),
            P(None, section),
        ),
        out_specs=(
            P(section + narrow, None),
            P(section + narrow, None),
            P(narrow, None, section),
            P(narrow, section, None),
            P(narrow, section),
        ),
        check_vma=False,
    )
```

```python
import jax
import jax.numpy as jnp
from jax import lax
from jax.sharding import Mesh, PartitionSpec as P

Y, XL, CORE, Z, XH = "y", "xl", "c", "z", "xh"
BF16 = jnp.bfloat16
F32 = jnp.float32
TIE = True


def shift(value, axis, by):
    n = lax.axis_size(axis)
    return lax.ppermute(value, axis, [(i, (i + by) % n) for i in range(n)])


def add(*terms):
    total = terms[0].astype(F32)
    for term in terms[1:]:
        total = total + term.astype(F32)
    return total


def tie(*groups):
    if not TIE:
        return groups
    return lax.optimization_barrier(groups)


def scatter_sum(q, ring, pair, up, offload):
    q = [q[0], q[up % 4], q[2], q[-up % 4]]
    if offload:
        (a,) = yield [(q[2][1], ring, up)]
        one = add(q[1][1], a).astype(BF16)
        b, c, d = yield [(one, ring, up), (q[2][0], ring, -up), (q[3][1], pair, 1)]
        near = add(q[0][1], b).astype(BF16)
        below = add(q[3][0], c, d).astype(BF16)
    else:
        a, b = yield [(q[2][1], ring, up), (q[3][1], ring, -up)]
        one = add(q[1][1], a).astype(BF16)
        c, d = yield [(one, ring, up), (q[2][0], ring, -up)]
        near = add(q[0][1], b, c).astype(BF16)
        below = add(q[3][0], d).astype(BF16)
    e, f, g = yield [(near, pair, 1), (q[1][0], ring, up), (below, ring, -up)]
    return add(q[0][0], e, f, g)


def gather(own, ring, pair, up, offload):
    r01, r10, r30 = yield [(own, pair, 1), (own, ring, -up), (own, ring, up)]
    if offload:
        r20, r11, r31 = yield [(r30, ring, up), (r01, ring, -up), (r30, pair, 1)]
        (r21,) = yield [(r11, ring, -up)]
    else:
        r20, r11 = yield [(r30, ring, up), (r01, ring, -up)]
        r31, r21 = yield [(r01, ring, up), (r11, ring, -up)]
    rows = [[own, r01], [r10, r11], [r20, r21], [r30, r31]]
    return [rows[0], rows[up % 4], rows[2], rows[-up % 4]]


def advance(run, got, *earlier):
    sends = run.send(got)
    return [shift(late(value, *earlier), axis, by) for value, axis, by in sends]


def finish(run, got):
    try:
        run.send(got)
    except StopIteration as stop:
        return stop.value


def whole(run):
    got = None
    for _ in range(3):
        got = advance(run, got)
    return finish(run, got)


def late(value, *earlier):
    bound = jnp.asarray(1e30, F32)
    for x in earlier:
        over = lax.slice(x, (0, 0), (1, 1)).reshape(()).astype(F32) > bound
        value = jnp.where(over, jnp.zeros_like(value), value)
    return value


def flat(rows):
    return jnp.concatenate([value for row in rows for value in row], axis=0)


def relative(table, ring, pair):
    double = jnp.concatenate([table, table], axis=0)
    turned = lax.dynamic_slice_in_dim(double, lax.axis_index(ring), 4, axis=0)
    return jnp.where(lax.axis_index(pair) == 1, turned[:, ::-1], turned)


def gelu_tanh(values):
    return jax.nn.gelu(values, approximate=True)


def dot(left, right, left_dim, right_dim):
    return lax.dot_general(
        left, right, (((left_dim,), (right_dim,)), ((), ())), preferred_element_type=F32
    )


def shards(tokens, upstream, up_weight, down_weight, gate_values, chosen, counts):
    section_id = lax.axis_index((Y, XL, CORE))
    narrow_id = lax.axis_index((Z, XH))
    tok_dev = tokens.shape[0]
    experts, slots = chosen.shape
    up_own = up_weight[0]
    down_own = down_weight[0]
    up_oth = shift(up_own, CORE, 1)
    down_oth = shift(down_own, CORE, 1)
    gate_column = gate_values[0][:, None]
    alive = lax.broadcasted_iota(jnp.int32, (experts, slots), 1) < counts
    place = jnp.where(alive, chosen - section_id * (tok_dev * experts), -1)
    turned = relative(place.reshape(4, 2, slots), Z, XH).reshape(experts * slots)
    mine_alive = turned[:slots] >= 0

    def select(table):
        token = lax.broadcasted_iota(jnp.int32, (1, tok_dev), 1)
        hit = ((table - narrow_id * tok_dev)[:, None] == token) & (table >= 0)[:, None]
        return hit.astype(BF16)

    select_turned = select(turned)
    def blocks(array):
        return [[array[(2 * i + j) * slots:(2 * i + j + 1) * slots] for j in range(2)] for i in range(4)]

    def place_back(rows):
        return dot(select_turned, flat(rows), 0, 0).astype(BF16)

    def blocks(array):
        return [[array[(2 * i + j) * slots:(2 * i + j + 1) * slots] for j in range(2)] for i in range(4)]

    terms_tokens = dot(select_turned, tokens, 1, 0).astype(BF16)
    picked_mine = whole(scatter_sum(blocks(terms_tokens), Z, XH, 1, False)).astype(BF16)
    select_late = select(late(turned, picked_mine))
    terms_upstream = dot(select_late, upstream, 1, 0).astype(BF16)
    back_wide = whole(scatter_sum(blocks(terms_upstream), Z, XH, 1, False))
    out_grad_mine = (gate_column * back_wide).astype(BF16)
    picked = whole(gather(picked_mine, Y, XL, 1, True))
    picked[0][0] = late(picked[0][0], out_grad_mine)
    picked = lax.optimization_barrier(flat(picked))
    spread = gather(out_grad_mine, Y, XL, -1, True)
    near = advance(spread, None)
    pre_own = dot(picked, up_own, 1, 0)
    pre_oth = dot(picked, up_oth, 1, 0)
    hid_own = gelu_tanh(pre_own).astype(BF16)
    hid_oth = gelu_tanh(pre_oth).astype(BF16)
    out_terms = add(dot(hid_own, down_own, 1, 0), dot(hid_oth, down_oth, 1, 0)).astype(BF16)
    summed = scatter_sum(blocks(out_terms), Y, XL, 1, True)
    first = advance(summed, None)
    near = advance(spread, near, out_terms)
    second = advance(summed, first)
    near = advance(spread, near)
    out_grad = lax.optimization_barrier(flat(finish(spread, near)))
    third = advance(summed, second)
    out_sum = finish(summed, third)
    gate_grad = jnp.sum(back_wide * out_sum, axis=1)[None, :]
    pg_own = jax.vjp(gelu_tanh, pre_own)[1](dot(out_grad, down_own, 1, 1))[0].astype(BF16)
    pg_oth = jax.vjp(gelu_tanh, pre_oth)[1](dot(out_grad, down_oth, 1, 1))[0].astype(BF16)
    pg_terms = add(dot(pg_own, up_own, 1, 1), dot(pg_oth, up_oth, 1, 1)).astype(BF16)
    contrib = jnp.where(mine_alive[:, None], gate_column * out_sum, 0.0).astype(BF16)
    contrib = late(contrib, pg_terms)
    summed = scatter_sum(blocks(pg_terms), Y, XL, -1, True)
    given = gather(contrib, Z, XH, 1, False)
    first = advance(summed, None)
    one = advance(given, None)
    second = advance(summed, first, one[1])
    two = advance(given, one)
    third = advance(summed, second, two[0])
    three = advance(given, two)
    layer_out = dot(select_turned, flat(finish(given, three)), 0, 0).astype(BF16)
    picked_grad = finish(summed, third).astype(BF16)
    def both(rows, others):
        return jnp.concatenate([rows, shift(others, CORE, 1)], axis=0)

    down_grad = dot(both(hid_own, hid_oth), both(out_grad, out_grad), 0, 0).astype(BF16)
    up_grad = dot(both(picked, picked), both(pg_own, pg_oth), 0, 0).astype(BF16)
    given = gather(picked_grad, Z, XH, 1, False)
    one = advance(given, None)
    two = advance(given, one, up_grad)
    three = advance(given, two, down_grad)
    token_grad = dot(select_turned, flat(finish(given, three)), 0, 0).astype(BF16)
    return (layer_out, token_grad, up_grad[None], down_grad[None], gate_grad)


def solution(mesh):
    fine = Mesh(mesh.devices.reshape(4, 2, 2, 4, 2), (Y, XL, CORE, Z, XH))
    section, narrow = (Y, XL, CORE), (Z, XH)
    return jax.shard_map(
        shards,
        mesh=fine,
        in_specs=(
            P(section + narrow, None),
            P(section + narrow, None),
            P(narrow, None, section),
            P(narrow, section, None),
            P(narrow, section),
            P(None, section),
            P(None, section),
        ),
        out_specs=(
            P(section + narrow, None),
            P(section + narrow, None),
            P(narrow, None, section),
            P(narrow, section, None),
            P(narrow, section),
        ),
        check_vma=False,
    )
```

```python
import jax
import jax.numpy as jnp
from jax import lax
from jax.sharding import Mesh, PartitionSpec as P

Y, XL, CORE, Z, XH = "y", "xl", "c", "z", "xh"
BF16 = jnp.bfloat16
F32 = jnp.float32
TIE = True


def shift(value, axis, by):
    n = lax.axis_size(axis)
    return lax.ppermute(value, axis, [(i, (i + by) % n) for i in range(n)])


def add(*terms):
    total = terms[0].astype(F32)
    for term in terms[1:]:
        total = total + term.astype(F32)
    return total


def tie(*groups):
    if not TIE:
        return groups
    return lax.optimization_barrier(groups)


def scatter_sum(q, ring, pair, up, offload):
    q = [q[0], q[up % 4], q[2], q[-up % 4]]
    if offload:
        (a,) = yield [(q[2][1], ring, up)]
        one = add(q[1][1], a).astype(BF16)
        b, c, d = yield [(one, ring, up), (q[2][0], ring, -up), (q[3][1], pair, 1)]
        near = add(q[0][1], b).astype(BF16)
        below = add(q[3][0], c, d).astype(BF16)
    else:
        a, b = yield [(q[2][1], ring, up), (q[3][1], ring, -up)]
        one = add(q[1][1], a).astype(BF16)
        c, d = yield [(one, ring, up), (q[2][0], ring, -up)]
        near = add(q[0][1], b, c).astype(BF16)
        below = add(q[3][0], d).astype(BF16)
    e, f, g = yield [(near, pair, 1), (q[1][0], ring, up), (below, ring, -up)]
    return add(q[0][0], e, f, g)


def gather(own, ring, pair, up, offload):
    r01, r10, r30 = yield [(own, pair, 1), (own, ring, -up), (own, ring, up)]
    if offload:
        r20, r11, r31 = yield [(r30, ring, up), (r01, ring, -up), (r30, pair, 1)]
        (r21,) = yield [(r11, ring, -up)]
    else:
        r20, r11 = yield [(r30, ring, up), (r01, ring, -up)]
        r31, r21 = yield [(r01, ring, up), (r11, ring, -up)]
    rows = [[own, r01], [r10, r11], [r20, r21], [r30, r31]]
    return [rows[0], rows[up % 4], rows[2], rows[-up % 4]]


def advance(run, got, ties=()):
    sends = [list(send) for send in run.send(got)]
    for number, earlier in ties:
        sends[number][0] = late(sends[number][0], earlier)
    return [shift(*send) for send in sends]


def finish(run, got):
    try:
        run.send(got)
    except StopIteration as stop:
        return stop.value


def whole(run):
    got = None
    for _ in range(3):
        got = advance(run, got)
    return finish(run, got)


def late(value, *earlier):
    for x in earlier:
        value = jnp.where(x > 1e30, jnp.zeros_like(value), value)
    return value


def flat(rows):
    return jnp.concatenate([value for row in rows for value in row], axis=0)


def relative(table, ring, pair):
    double = jnp.concatenate([table, table], axis=0)
    turned = lax.dynamic_slice_in_dim(double, lax.axis_index(ring), 4, axis=0)
    return jnp.where(lax.axis_index(pair) == 1, turned[:, ::-1], turned)


def gelu_tanh(values):
    return jax.nn.gelu(values, approximate=True)


def dot(left, right, left_dim, right_dim):
    return lax.dot_general(
        left, right, (((left_dim,), (right_dim,)), ((), ())), preferred_element_type=F32
    )


def shards(tokens, upstream, up_weight, down_weight, gate_values, chosen, counts):
    section_id = lax.axis_index((Y, XL, CORE))
    narrow_id = lax.axis_index((Z, XH))
    tok_dev = tokens.shape[0]
    experts, slots = chosen.shape
    up_own = up_weight[0]
    down_own = down_weight[0]
    up_oth = shift(up_own, CORE, 1)
    down_oth = shift(down_own, CORE, 1)
    gate_column = gate_values[0][:, None]
    alive = lax.broadcasted_iota(jnp.int32, (experts, slots), 1) < counts
    place = jnp.where(alive, chosen - section_id * (tok_dev * experts), -1)
    turned = relative(place.reshape(4, 2, slots), Z, XH).reshape(experts * slots)
    mine_alive = turned[:slots] >= 0

    def select(table):
        token = lax.broadcasted_iota(jnp.int32, (1, tok_dev), 1)
        hit = ((table - narrow_id * tok_dev)[:, None] == token) & (table >= 0)[:, None]
        return hit.astype(BF16)

    select_turned = select(turned)
    def blocks(array):
        return [[array[(2 * i + j) * slots:(2 * i + j + 1) * slots] for j in range(2)] for i in range(4)]

    def place_back(rows):
        return dot(select_turned, flat(rows), 0, 0).astype(BF16)

    def blocks(array):
        return [[array[(2 * i + j) * slots:(2 * i + j + 1) * slots] for j in range(2)] for i in range(4)]

    terms_tokens = dot(select_turned, tokens, 1, 0).astype(BF16)
    picked_mine = whole(scatter_sum(blocks(terms_tokens), Z, XH, 1, False)).astype(BF16)
    terms_upstream = dot(select_turned, upstream, 1, 0).astype(BF16)
    spread = gather(picked_mine, Y, XL, 1, True)
    summed = scatter_sum(blocks(terms_upstream), Z, XH, 1, False)
    t1 = advance(spread, None)
    u1 = advance(summed, None, [(0, picked_mine), (1, picked_mine)])
    t2 = advance(spread, t1)
    u2 = advance(summed, u1, [(0, t1[1])])
    t3 = advance(spread, t2, [(0, u1[0])])
    u3 = advance(summed, u2, [(0, t2[0]), (2, t2[0])])
    picked = finish(spread, t3)
    picked[0][0] = late(picked[0][0], u3[0])
    picked = lax.optimization_barrier(flat(picked))
    back_wide = finish(summed, u3)
    out_grad_mine = (gate_column * back_wide).astype(BF16)
    pre_own = dot(picked, up_own, 1, 0)
    pre_oth = dot(picked, up_oth, 1, 0)
    hid_own = gelu_tanh(pre_own).astype(BF16)
    hid_oth = gelu_tanh(pre_oth).astype(BF16)
    out_terms = add(dot(hid_own, down_own, 1, 0), dot(hid_oth, down_oth, 1, 0)).astype(BF16)
    summed = scatter_sum(blocks(out_terms), Y, XL, 1, True)
    spread = gather(out_grad_mine, Y, XL, -1, True)
    u1 = advance(spread, None)
    t1 = advance(summed, None)
    u2 = advance(spread, u1, [(1, t1[0]), (0, t1[0]), (2, t1[0])])
    t2 = advance(summed, t1)
    u3 = advance(spread, u2, [(0, t2[0])])
    t3 = advance(summed, t2, [(0, u1[0]), (2, u1[0])])
    out_grad = lax.optimization_barrier(flat(finish(spread, u3)))
    out_sum = finish(summed, t3)
    gate_grad = jnp.sum(back_wide * out_sum, axis=1)[None, :]
    pg_own = jax.vjp(gelu_tanh, pre_own)[1](dot(out_grad, down_own, 1, 1))[0].astype(BF16)
    pg_oth = jax.vjp(gelu_tanh, pre_oth)[1](dot(out_grad, down_oth, 1, 1))[0].astype(BF16)
    pg_terms = add(dot(pg_own, up_own, 1, 1), dot(pg_oth, up_oth, 1, 1)).astype(BF16)
    contrib = jnp.where(mine_alive[:, None], gate_column * out_sum, 0.0).astype(BF16)
    contrib = late(contrib, pg_terms[:slots])
    summed = scatter_sum(blocks(pg_terms), Y, XL, -1, True)
    given = gather(contrib, Z, XH, 1, False)
    u1 = advance(summed, None)
    t1 = advance(given, None)
    u2 = advance(summed, u1)
    t2 = advance(given, t1, [(1, u1[0])])
    u3 = advance(summed, u2, [(0, t2[0]), (2, t2[0])])
    t3 = advance(given, t2)
    layer_out = dot(select_turned, flat(finish(given, t3)), 0, 0).astype(BF16)
    picked_grad = finish(summed, u3).astype(BF16)
    def both(rows, others):
        return jnp.concatenate([rows, shift(others, CORE, 1)], axis=0)

    down_grad = dot(both(hid_own, hid_oth), both(out_grad, out_grad), 0, 0).astype(BF16)
    up_grad = dot(both(picked, picked), both(pg_own, pg_oth), 0, 0).astype(BF16)
    given = gather(picked_grad, Z, XH, 1, False)
    u1 = advance(given, None)
    u2 = advance(given, u1, [(1, t2[0])])
    u3 = advance(given, u2, [(1, down_grad[:slots])])
    token_grad = dot(select_turned, flat(finish(given, u3)), 0, 0).astype(BF16)
    return (layer_out, token_grad, up_grad[None], down_grad[None], gate_grad)


def solution(mesh):
    fine = Mesh(mesh.devices.reshape(4, 2, 2, 4, 2), (Y, XL, CORE, Z, XH))
    section, narrow = (Y, XL, CORE), (Z, XH)
    return jax.shard_map(
        shards,
        mesh=fine,
        in_specs=(
            P(section + narrow, None),
            P(section + narrow, None),
            P(narrow, None, section),
            P(narrow, section, None),
            P(narrow, section),
            P(None, section),
            P(None, section),
        ),
        out_specs=(
            P(section + narrow, None),
            P(section + narrow, None),
            P(narrow, None, section),
            P(narrow, section, None),
            P(narrow, section),
        ),
        check_vma=False,
    )
```

```python
import jax
import jax.numpy as jnp
from jax import lax
from jax.sharding import Mesh, PartitionSpec as P

Y, XL, CORE, Z, XH = "y", "xl", "c", "z", "xh"
BF16 = jnp.bfloat16
F32 = jnp.float32
TIE = True


def shift(value, axis, by):
    n = lax.axis_size(axis)
    return lax.ppermute(value, axis, [(i, (i + by) % n) for i in range(n)])


def add(*terms):
    total = terms[0].astype(F32)
    for term in terms[1:]:
        total = total + term.astype(F32)
    return total


def tie(*groups):
    if not TIE:
        return groups
    return lax.optimization_barrier(groups)


def scatter_sum(q, ring, pair, up, offload):
    q = [q[0], q[up % 4], q[2], q[-up % 4]]
    if offload:
        (a,) = yield [(q[2][1], ring, up)]
        one = add(q[1][1], a).astype(BF16)
        b, c, d = yield [(one, ring, up), (q[2][0], ring, -up), (q[3][1], pair, 1)]
        near = add(q[0][1], b).astype(BF16)
        below = add(q[3][0], c, d).astype(BF16)
    else:
        a, b = yield [(q[2][1], ring, up), (q[3][1], ring, -up)]
        one = add(q[1][1], a).astype(BF16)
        c, d = yield [(one, ring, up), (q[2][0], ring, -up)]
        near = add(q[0][1], b, c).astype(BF16)
        below = add(q[3][0], d).astype(BF16)
    e, f, g = yield [(near, pair, 1), (q[1][0], ring, up), (below, ring, -up)]
    return add(q[0][0], e, f, g)


def gather(own, ring, pair, up, offload):
    r01, r10, r30 = yield [(own, pair, 1), (own, ring, -up), (own, ring, up)]
    if offload:
        r20, r11, r31 = yield [(r30, ring, up), (r01, ring, -up), (r30, pair, 1)]
        (r21,) = yield [(r11, ring, -up)]
    else:
        r20, r11 = yield [(r30, ring, up), (r01, ring, -up)]
        r31, r21 = yield [(r01, ring, up), (r11, ring, -up)]
    rows = [[own, r01], [r10, r11], [r20, r21], [r30, r31]]
    return [rows[0], rows[up % 4], rows[2], rows[-up % 4]]


def advance(run, got, ties=()):
    sends = [list(send) for send in run.send(got)]
    for number, earlier in ties:
        sends[number][0] = late(sends[number][0], earlier)
    return [shift(*send) for send in sends]


def finish(run, got):
    try:
        run.send(got)
    except StopIteration as stop:
        return stop.value


def whole(run):
    got = None
    for _ in range(3):
        got = advance(run, got)
    return finish(run, got)


def late(value, *earlier):
    for x in earlier:
        value = jnp.where(x > 1e30, jnp.zeros_like(value), value)
    return value


def flat(rows):
    return jnp.concatenate([value for row in rows for value in row], axis=0)


def relative(table, ring, pair):
    double = jnp.concatenate([table, table], axis=0)
    turned = lax.dynamic_slice_in_dim(double, lax.axis_index(ring), 4, axis=0)
    return jnp.where(lax.axis_index(pair) == 1, turned[:, ::-1], turned)


def gelu_tanh(values):
    return jax.nn.gelu(values, approximate=True)


def dot(left, right, left_dim, right_dim):
    return lax.dot_general(
        left, right, (((left_dim,), (right_dim,)), ((), ())), preferred_element_type=F32
    )


def shards(tokens, upstream, up_weight, down_weight, gate_values, chosen, counts):
    section_id = lax.axis_index((Y, XL, CORE))
    narrow_id = lax.axis_index((Z, XH))
    tok_dev = tokens.shape[0]
    experts, slots = chosen.shape
    up_own = up_weight[0]
    down_own = down_weight[0]
    up_oth = shift(up_own, CORE, 1)
    down_oth = shift(down_own, CORE, 1)
    gate_column = gate_values[0][:, None]
    alive = lax.broadcasted_iota(jnp.int32, (experts, slots), 1) < counts
    place = jnp.where(alive, chosen - section_id * (tok_dev * experts), -1)
    turned = relative(place.reshape(4, 2, slots), Z, XH).reshape(experts * slots)
    mine_alive = turned[:slots] >= 0

    def select(table):
        token = lax.broadcasted_iota(jnp.int32, (1, tok_dev), 1)
        hit = ((table - narrow_id * tok_dev)[:, None] == token) & (table >= 0)[:, None]
        return hit.astype(BF16)

    select_turned = select(turned)
    def blocks(array):
        return [[array[(2 * i + j) * slots:(2 * i + j + 1) * slots] for j in range(2)] for i in range(4)]

    def place_back(rows):
        return dot(select_turned, flat(rows), 0, 0).astype(BF16)

    def blocks(array):
        return [[array[(2 * i + j) * slots:(2 * i + j + 1) * slots] for j in range(2)] for i in range(4)]

    terms_tokens = dot(select_turned, tokens, 1, 0).astype(BF16)
    picked_mine = whole(scatter_sum(blocks(terms_tokens), Z, XH, 1, False)).astype(BF16)
    terms_upstream = dot(select_turned, upstream, 1, 0).astype(BF16)
    spread = gather(picked_mine, Y, XL, 1, True)
    summed = scatter_sum(blocks(terms_upstream), Z, XH, 1, False)
    t1 = advance(spread, None)
    u1 = advance(summed, None, [(0, picked_mine), (1, picked_mine)])
    t2 = advance(spread, t1)
    u2 = advance(summed, u1, [(0, t1[1])])
    t3 = advance(spread, t2)
    u3 = advance(summed, u2, [(0, t2[0]), (2, t2[0])])
    picked = finish(spread, t3)
    picked[0][0] = late(picked[0][0], u3[0])
    picked = lax.optimization_barrier(flat(picked))
    back_wide = finish(summed, u3)
    out_grad_mine = (gate_column * back_wide).astype(BF16)
    pre_own = dot(picked, up_own, 1, 0)
    pre_oth = dot(picked, up_oth, 1, 0)
    hid_own = gelu_tanh(pre_own).astype(BF16)
    hid_oth = gelu_tanh(pre_oth).astype(BF16)
    out_terms = add(dot(hid_own, down_own, 1, 0), dot(hid_oth, down_oth, 1, 0)).astype(BF16)
    summed = scatter_sum(blocks(out_terms), Y, XL, 1, True)
    spread = gather(out_grad_mine, Y, XL, -1, True)
    u1 = advance(spread, None)
    t1 = advance(summed, None)
    u2 = advance(spread, u1, [(1, t1[0]), (0, t1[0]), (2, t1[0])])
    t2 = advance(summed, t1)
    u3 = advance(spread, u2, [(0, t2[0])])
    t3 = advance(summed, t2, [(0, u1[0]), (2, u1[0])])
    out_grad = lax.optimization_barrier(flat(finish(spread, u3)))
    out_sum = finish(summed, t3)
    gate_grad = jnp.sum(back_wide * out_sum, axis=1)[None, :]
    pg_own = jax.vjp(gelu_tanh, pre_own)[1](dot(out_grad, down_own, 1, 1))[0].astype(BF16)
    pg_oth = jax.vjp(gelu_tanh, pre_oth)[1](dot(out_grad, down_oth, 1, 1))[0].astype(BF16)
    pg_terms = add(dot(pg_own, up_own, 1, 1), dot(pg_oth, up_oth, 1, 1)).astype(BF16)
    contrib = jnp.where(mine_alive[:, None], gate_column * out_sum, 0.0).astype(BF16)
    contrib = late(contrib, pg_terms[:slots])
    summed = scatter_sum(blocks(pg_terms), Y, XL, -1, True)
    given = gather(contrib, Z, XH, 1, False)
    u1 = advance(summed, None)
    t1 = advance(given, None)
    u2 = advance(summed, u1)
    t2 = advance(given, t1, [(1, u1[0])])
    u3 = advance(summed, u2, [(0, t2[0]), (2, t2[0])])
    t3 = advance(given, t2)
    layer_out = dot(select_turned, flat(finish(given, t3)), 0, 0).astype(BF16)
    picked_grad = finish(summed, u3).astype(BF16)
    def both(rows, others):
        return jnp.concatenate([rows, shift(others, CORE, 1)], axis=0)

    down_grad = dot(both(hid_own, hid_oth), both(out_grad, out_grad), 0, 0).astype(BF16)
    up_grad = dot(both(picked, picked), both(pg_own, pg_oth), 0, 0).astype(BF16)
    given = gather(picked_grad, Z, XH, 1, False)
    u1 = advance(given, None)
    u2 = advance(given, u1, [(1, t2[0])])
    u3 = advance(given, u2, [(1, down_grad[:slots])])
    token_grad = dot(select_turned, flat(finish(given, u3)), 0, 0).astype(BF16)
    return (layer_out, token_grad, up_grad[None], down_grad[None], gate_grad)


def solution(mesh):
    fine = Mesh(mesh.devices.reshape(4, 2, 2, 4, 2), (Y, XL, CORE, Z, XH))
    section, narrow = (Y, XL, CORE), (Z, XH)
    return jax.shard_map(
        shards,
        mesh=fine,
        in_specs=(
            P(section + narrow, None),
            P(section + narrow, None),
            P(narrow, None, section),
            P(narrow, section, None),
            P(narrow, section),
            P(None, section),
            P(None, section),
        ),
        out_specs=(
            P(section + narrow, None),
            P(section + narrow, None),
            P(narrow, None, section),
            P(narrow, section, None),
            P(narrow, section),
        ),
        check_vma=False,
    )
```
